512 devices in a mesh: dp: 32 (over z_hi, y, core), mp: 16 (over x, z_lo).
Axes of the slice: x: 4, y: 8, z: 8 (z_hi: 2, z_lo: 4; z = z_hi * 4 + z_lo), core: 2. Of those that a mesh axis runs over, the one named last changes fastest.
Arguments:
- tokens: bfloat16 [8192, 3072], P('dp', 'mp'), may hold values from -192 to 192
- w_query: bfloat16 [3072, 3072], P('dp', 'mp'), may hold values from -0.109375 to 0.109375
- w_key: bfloat16 [3072, 3072], P('dp', 'mp'), may hold values from -0.109375 to 0.109375
- w_value: bfloat16 [3072, 3072], P('dp', 'mp'), may hold values from -0.109375 to 0.109375
- w_out: bfloat16 [3072, 3072], P('mp'), may hold values from -0.109375 to 0.109375
- cotangent: bfloat16 [8192, 3072], P('dp', 'mp'), may hold values from -0.59765625 to 0.59765625
Outputs:
- branch_out: bfloat16 [8192, 3072], P('dp', 'mp')
- grad_query: float32 [3072, 3072], P('dp', 'mp')
- grad_key: float32 [3072, 3072], P('dp', 'mp')
- grad_value: float32 [3072, 3072], P('dp', 'mp')
- grad_out: float32 [3072, 3072], P('mp')
The draws below stay inside these ranges and needn't reach their ends.
All inputs are finite; a program needn't handle non-finite values.
Results may differ from the reference program's by a relative error of at most 0.034.
Values may be sent and summed in bfloat16 or wider, within the bound.
A program may use at most 64 MiB of HBM per device.

```python
import jax
import jax.numpy as jnp
from jax import lax

D = 3072
HEADS = 48
HEAD_DIM = 64
TOK = 128
IMGS = 2
INNER = 3072
TOKENS = 8192
N_DP = 32


def draw_tokens(key, part):
    key = jax.random.fold_in(key, 11)
    base_key, col_key, row_key = jax.random.split(key, 3)
    position = jnp.arange(D, dtype=jnp.float32) / D
    col_scale = jnp.exp(jnp.log(3.0) * position + jax.random.uniform(col_key, (D,), jnp.float32, 0.0, jnp.log(10.0)))
    base = jax.random.normal(base_key, (TOKENS, D), jnp.float32)
    row_scale = jnp.exp(jax.random.uniform(row_key, (TOKENS, 1), jnp.float32, 0.0, jnp.log(10.0)))
    base = jnp.clip(base, -4.0, 4.0)
    return (0.1 * base * row_scale * col_scale).astype(jnp.bfloat16)


def shard_levels(rng, extent, cuts, least, high):
    def one(dim, shards_of):
        draws = jax.random.uniform(jax.random.fold_in(jax.random.fold_in(rng, 6), dim), (shards_of,), jnp.float32, least / len(cuts), high / len(cuts))
        return jnp.repeat(jnp.exp(draws), extent[dim] // shards_of).reshape((-1,) + (1,) * (len(extent) - dim - 1))

    loudness = one(*cuts[0])
    for cut in cuts[1:]:
        loudness = loudness * one(*cut)
    return loudness


def bell_draw(own_key, dims, scale, reach, cuts=(), kind=jnp.bfloat16):
    values = jax.random.normal(own_key, dims, jnp.float32) * scale
    if len(cuts) > 0:
        values = shard_levels(own_key, dims, cuts, -0.22, 0.18) * values
    return jnp.clip(values, min=-reach, max=reach).astype(kind)


def setup_inputs(seed: int = 0) -> dict:
    arg_keys = jax.random.split(jax.random.key(seed), 7)
    return {
        "tokens": draw_tokens(jax.random.fold_in(arg_keys[6], 71), 0),
        "w_query": bell_draw(arg_keys[1], (D, INNER), D ** -0.5, 0.109375, ((0, 32), (1, 16))),
        "w_key": bell_draw(arg_keys[2], (D, INNER), D ** -0.5, 0.109375, ((0, 32), (1, 16))),
        "w_value": bell_draw(arg_keys[3], (D, INNER), D ** -0.5, 0.109375, ((0, 32), (1, 16))),
        "w_out": bell_draw(arg_keys[4], (D, INNER), INNER ** -0.5, 0.109375, ((0, 16),)),
        "cotangent": bell_draw(arg_keys[5], (TOKENS, D), 0.1, 0.59765625, ((0, 32), (1, 16))),
    }


EPS = 1e-06

def row_norm(values):
    mean = lax.optimization_barrier(jnp.mean(values, axis=-1, keepdims=True))
    centred = values - mean
    var = lax.optimization_barrier(jnp.mean(centred * centred, axis=-1, keepdims=True))
    return centred * lax.rsqrt(var + EPS)

def head_norm(projected):
    mean = lax.optimization_barrier(jnp.mean(projected, axis=-1, keepdims=True))
    centred = projected - mean
    var = lax.optimization_barrier(jnp.mean(centred * centred, axis=-1, keepdims=True))
    inverse = lax.rsqrt(var + EPS)
    return (centred * inverse, inverse)

def rounded(values):
    return lax.optimization_barrier(values.astype(jnp.bfloat16)).astype(jnp.float32)

def attend(q_low, k_low, v_low):
    scale = HEAD_DIM ** (-0.5)
    scores = jnp.einsum('gthd,gshd->ghts', q_low.astype(jnp.float32), k_low.astype(jnp.float32)) * scale
    weights = jnp.exp(scores)
    probs = weights / lax.optimization_barrier(jnp.sum(weights, axis=-1, keepdims=True))
    probs_low = probs.astype(jnp.bfloat16)
    mixed = jnp.einsum('ghts,gshd->gthd', probs_low.astype(jnp.float32), v_low.astype(jnp.float32))
    return (probs, probs_low, mixed.astype(jnp.bfloat16))

def norm_back(grad_hat, hat, inverse):
    first = lax.optimization_barrier(jnp.mean(grad_hat, axis=-1, keepdims=True))
    second = lax.optimization_barrier(jnp.mean(grad_hat * hat, axis=-1, keepdims=True))
    return inverse * (grad_hat - first - hat * second)

def attend_back(q_low, k_low, v_low, probs, probs_low, d_att, q_hat, inv_q, k_hat, inv_k):
    scale = HEAD_DIM ** (-0.5)
    d_att32 = d_att.astype(jnp.float32)
    d_probs = jnp.einsum('gthd,gshd->ghts', d_att32, v_low.astype(jnp.float32))
    inner_sum = lax.optimization_barrier(jnp.sum(probs * d_probs, axis=-1, keepdims=True))
    d_scores = (probs * (d_probs - inner_sum) * scale).astype(jnp.bfloat16).astype(jnp.float32)
    d_qhat = jnp.einsum('ghts,gshd->gthd', d_scores, k_low.astype(jnp.float32))
    d_khat = jnp.einsum('ghts,gthd->gshd', d_scores, q_low.astype(jnp.float32))
    d_vfull = jnp.einsum('ghts,gthd->gshd', probs_low.astype(jnp.float32), d_att32)
    d_query = norm_back(d_qhat, q_hat, inv_q).astype(jnp.bfloat16)
    d_key = norm_back(d_khat, k_hat, inv_k).astype(jnp.bfloat16)
    return (d_query, d_key, d_vfull.astype(jnp.bfloat16))

def reference(tokens, w_query, w_key, w_value, w_out, cotangent):
    groups = tokens.reshape(N_DP, IMGS * TOK, D)
    cot_groups = cotangent.reshape(N_DP, IMGS * TOK, D)
    shape4 = (IMGS, TOK, HEADS, HEAD_DIM)
    rows = IMGS * TOK

    def one_group(carry, inputs):
        acc_query, acc_key, acc_value, acc_out = carry
        image, cot = inputs
        x_norm = row_norm(image.astype(jnp.float32)).astype(jnp.bfloat16)
        query = jnp.dot(x_norm, w_query, preferred_element_type=jnp.float32).reshape(shape4)
        key = jnp.dot(x_norm, w_key, preferred_element_type=jnp.float32).reshape(shape4)
        value = jnp.dot(x_norm, w_value, preferred_element_type=jnp.float32).reshape(shape4)
        q_hat, inv_q = head_norm(query)
        k_hat, inv_k = head_norm(key)
        q_low = q_hat.astype(jnp.bfloat16)
        k_low = k_hat.astype(jnp.bfloat16)
        v_low = value.astype(jnp.bfloat16)
        probs, probs_low, mixed = attend(q_low, k_low, v_low)
        attended = mixed.reshape(rows, INNER)
        branch = jnp.dot(attended, w_out.T, preferred_element_type=jnp.float32).astype(jnp.bfloat16)
        term_out = rounded(jnp.dot(cot.T, attended, preferred_element_type=jnp.float32))
        d_att = jnp.dot(cot, w_out, preferred_element_type=jnp.float32).astype(jnp.bfloat16)
        d_query, d_key, d_value = attend_back(q_low, k_low, v_low, probs, probs_low, d_att.reshape(shape4), q_hat, inv_q, k_hat, inv_k)
        term_query = rounded(jnp.dot(x_norm.T, d_query.reshape(rows, INNER), preferred_element_type=jnp.float32))
        term_key = rounded(jnp.dot(x_norm.T, d_key.reshape(rows, INNER), preferred_element_type=jnp.float32))
        term_value = rounded(jnp.dot(x_norm.T, d_value.reshape(rows, INNER), preferred_element_type=jnp.float32))
        carry = (acc_query + term_query, acc_key + term_key, acc_value + term_value, acc_out + term_out)
        return (carry, branch)
    start = (jnp.zeros((D, INNER), jnp.float32), jnp.zeros((D, INNER), jnp.float32), jnp.zeros((D, INNER), jnp.float32), jnp.zeros((D, INNER), jnp.float32))
    totals, branches = lax.scan(one_group, start, (groups, cot_groups))
    branch_out = branches.reshape(TOKENS, D)
    return (branch_out, totals[0], totals[1], totals[2], totals[3])
```

```python
import functools

import jax
import jax.numpy as jnp
from jax import lax
from jax.experimental import pallas as pl
from jax.experimental.pallas import tpu as pltpu
from jax.sharding import PartitionSpec as P

HEAD_DIM = 64
TOK = 128
EPS = 1e-06

NZH, NY, NC = 2, 8, 2
NX, NZ = 4, 4
ROWS = 256
LOCAL = 192
PACK = 384
HALF = PACK // 2
WROWS = 96
WCOLS = 640
GCOLS = 384
F32 = jnp.float32
BF16 = jnp.bfloat16
MESH = pl.DeviceIdType.MESH
VMEM = pltpu.CompilerParams


def wrap(value, size):
    return lax.rem(value + size, size)


class Place:
    def __init__(self):
        dp, mp = lax.axis_index("dp"), lax.axis_index("mp")
        self.dp, self.mp = dp, mp
        self.zh = lax.div(dp, NY * NC)
        self.y = lax.rem(lax.div(dp, NC), NY)
        self.c = lax.rem(dp, NC)
        self.x = lax.div(mp, NZ)
        self.z = lax.rem(mp, NZ)

    def on_mp(self, x, z):
        return (self.dp, x * NZ + z)

    def on_dp(self, zh, y, c):
        return (zh * (NY * NC) + y * NC + c, self.mp)

    def x_side(self, step):
        return self.on_mp(wrap(self.x + step, NX), self.z)

    def z_peer(self, step):
        return self.on_mp(self.x, wrap(self.z + step, NZ))

    def y_side(self, step):
        return self.on_dp(self.zh, wrap(self.y + step, NY), self.c)

    def zh_peer(self):
        return self.on_dp(1 - self.zh, self.y, self.c)

    def sibling(self):
        return self.on_dp(self.zh, self.y, 1 - self.c)


class Links:
    def __init__(self, send, recv):
        self.send, self.recv, self.count, self.started = send, recv, 0, []

    def copy(self, src, dst, device):
        i = self.count
        self.count += 1
        one = pltpu.make_async_remote_copy(
            src_ref=src,
            dst_ref=dst,
            send_sem=self.send.at[i],
            recv_sem=self.recv.at[i],
            device_id=device,
            device_id_type=MESH,
        )
        one.start()
        self.started.append(one)
        return one

    def finish(self):
        for one in self.started:
            one.wait_send()


def greet(devices):
    barrier = pltpu.get_barrier_semaphore()
    for device in devices:
        pl.semaphore_signal(barrier, inc=1, device_id=device, device_id_type=MESH)
    pl.semaphore_wait(barrier, len(devices))


def pack_into(ref, index, block):
    ref[index + (slice(0, 256), slice(None))] = block[:, 0:128]
    ref[index + (slice(256, 384), slice(0, 64))] = block[0:128, 128:192]
    ref[index + (slice(256, 384), slice(64, 128))] = block[128:256, 128:192]


def unpack_into(ref, column, packed):
    ref[:, column : column + 128] = packed[0:256]
    ref[0:128, column + 128 : column + 192] = packed[256:384, 0:64]
    ref[128:256, column + 128 : column + 192] = packed[256:384, 64:128]


def gather_mp(at, links, buf):
    x, z = at.x, at.z
    own = buf.at[x, z]
    peers = [links.copy(own, own, at.z_peer(k)) for k in (1, 2, 3)]
    rights, lefts, fars = [], [], []

    def sides(zz):
        piece = buf.at[x, zz]
        rights.append(links.copy(piece, piece, at.x_side(1)))
        lefts.append(links.copy(piece, piece, at.x_side(-1)))

    sides(z)
    yield
    for k in (1, 2, 3):
        peers[k - 1].wait_recv()
        sides(wrap(z - k, NZ))
        yield
    for k in range(NZ):
        zz = wrap(z - k, NZ)
        rights[k].wait_recv()
        piece = buf.at[wrap(x - 1, NX), zz, pl.ds(0, HALF)]
        fars.append(links.copy(piece, piece, at.x_side(1)))
        yield
        lefts[k].wait_recv()
        piece = buf.at[wrap(x + 1, NX), zz, pl.ds(HALF, HALF)]
        fars.append(links.copy(piece, piece, at.x_side(-1)))
        yield
    for one in fars:
        one.wait_recv()
    yield


def reduce_mp(at, links, part, half_buf, side_buf, sums, peer_buf, finish):
    x, z = at.x, at.z
    right, left, far = wrap(x + 1, NX), wrap(x - 1, NX), wrap(x + 2, NX)
    low, high = pl.ds(0, HALF), pl.ds(HALF, HALF)
    halves = [
        links.copy(part.at[far, :, low], half_buf.at[0], at.x_side(1)),
        links.copy(part.at[far, :, high], half_buf.at[1], at.x_side(-1)),
    ]
    plain = [
        links.copy(part.at[right, :, high], side_buf.at[0, :, high], at.x_side(1)),
        links.copy(part.at[left, :, low], side_buf.at[1, :, low], at.x_side(-1)),
    ]
    yield
    halves[0].wait_recv()
    part[right, :, 0:HALF] = (part[right, :, 0:HALF].astype(F32) + half_buf[0].astype(F32)).astype(BF16)
    plain.append(links.copy(part.at[right, :, low], side_buf.at[0, :, low], at.x_side(1)))
    yield
    halves[1].wait_recv()
    part[left, :, HALF:PACK] = (part[left, :, HALF:PACK].astype(F32) + half_buf[1].astype(F32)).astype(BF16)
    plain.append(links.copy(part.at[left, :, high], side_buf.at[1, :, high], at.x_side(-1)))
    yield
    for one in plain:
        one.wait_recv()
    peers = []
    for k in (1, 2, 3):
        zz = wrap(z + k, NZ)
        total = part[x, zz].astype(F32) + side_buf[0, zz].astype(F32) + side_buf[1, zz].astype(F32)
        sums[k - 1] = total.astype(BF16)
        peers.append(links.copy(sums.at[k - 1], peer_buf.at[k - 1], at.z_peer(k)))
    total = part[x, z].astype(F32) + side_buf[0, z].astype(F32) + side_buf[1, z].astype(F32)
    yield
    for k in (1, 2, 3):
        peers[k - 1].wait_recv()
        total = total + peer_buf[k - 1].astype(F32)
    finish(total)
    yield


HOPS = ((4, 3), (3, 4))


def gather_y(at, links, piece_of, ready, also):
    y = at.y
    inbound = {}
    for q in (0, 1):
        ready(q)
        piece = piece_of(q, y)
        inbound[q, 0] = links.copy(piece, piece, at.y_side(1))
        inbound[q, 1] = links.copy(piece, piece, at.y_side(-1))
        also(q, y)
        yield
    for hop in (1, 2, 3, 4):
        for q in (0, 1):
            for side, step in ((0, 1), (1, -1)):
                if hop > HOPS[q][side]:
                    continue
                inbound[q, side].wait_recv()
                yy = wrap(y - step * hop, NY)
                piece = piece_of(q, yy)
                if hop < HOPS[q][side]:
                    inbound[q, side] = links.copy(piece, piece, at.y_side(step))
                also(q, yy)
                yield


def reduce_y(at, links, own, out_buf, in_buf, result):
    y = at.y
    inbound = {}
    slot = 0
    for dist in (4, 3, 2, 1):
        for q in (0, 1):
            for side, step in ((0, 1), (1, -1)):
                if dist > HOPS[q][side]:
                    continue
                total = own(q, wrap(y + step * dist, NY), (step * dist) % NY)
                if (q, side) in inbound:
                    before, one = inbound[q, side]
                    one.wait_recv()
                    total = total + in_buf[before].astype(F32)
                out_buf[slot] = total.astype(BF16)
                one = links.copy(out_buf.at[slot], in_buf.at[slot], at.y_side(step))
                inbound[q, side] = (slot, one)
                slot += 1
                yield
    for q in (0, 1):
        total = own(q, y, 0)
        for side in (0, 1):
            before, one = inbound[q, side]
            one.wait_recv()
            total = total + in_buf[before].astype(F32)
        result(q, total)
        yield


def gather_dp(at, links, buf):
    zh, y, c = at.zh, at.y, at.c
    own = buf.at[zh, y, c]
    across = links.copy(own, own, at.zh_peer())
    beside = []

    def piece_of(q, yy):
        return buf.at[zh if q == 0 else 1 - zh, yy, c]

    def ready(q):
        if q == 1:
            across.wait_recv()

    def also(q, yy):
        piece = piece_of(q, yy)
        beside.append(links.copy(piece, piece, at.sibling()))

    yield from gather_y(at, links, piece_of, ready, also)
    for one in beside:
        one.wait_recv()
    yield


def sibling_terms(at, links, src, buf):
    copies = {}
    for offset in (4, 3, 5, 2, 6, 1, 7, 0):
        yy = wrap(at.y + offset, NY)
        copies[offset] = links.copy(src(yy, 1 - at.c), buf.at[yy], at.sibling())
    waited = set()

    def arrived(offset):
        if offset not in waited:
            waited.add(offset)
            copies[offset].wait_recv()

    return arrived


def reduce_dp(at, links, terms, sib_buf, out_buf, in_buf, keep, send, peer_buf, finish):
    zh, c = at.zh, at.c
    arrived = sibling_terms(at, links, lambda yy, cc: terms.at[:, yy, cc], sib_buf)
    yield

    def own(q, yy, offset):
        arrived(offset)
        return terms[q, yy, c].astype(F32) + sib_buf[yy, q].astype(F32)

    def result(q, total):
        keep[q] = total
        send[q] = total.astype(BF16)

    yield from reduce_y(at, links, own, out_buf, in_buf, result)
    one = links.copy(send.at[1 - zh], peer_buf, at.zh_peer())
    yield
    one.wait_recv()
    finish(keep[zh] + peer_buf[...].astype(F32))
    yield


def allreduce_dp(at, links, terms, sib_buf, out_buf, in_buf, send, peer_buf, whole):
    y, c = at.y, at.c
    rows = WROWS // 2
    arrived = sibling_terms(at, links, lambda yy, cc: terms.at[cc, yy], sib_buf)
    yield

    def own(q, yy, offset):
        arrived(offset)
        here = pl.ds(q * rows, rows)
        return terms[c, yy, here].astype(F32) + sib_buf[yy, here].astype(F32)

    across, beside = [], []

    def result(q, total):
        send[q] = total.astype(BF16)
        across.append(links.copy(send.at[q], peer_buf.at[q], at.zh_peer()))

    yield from reduce_y(at, links, own, out_buf, in_buf, result)

    def piece_of(q, yy):
        return whole.at[c, yy, pl.ds(q * rows, rows)]

    def ready(q):
        across[q].wait_recv()
        total = send[q].astype(F32) + peer_buf[q].astype(F32)
        whole[c, y, q * rows : (q + 1) * rows] = total.astype(BF16)

    def also(q, yy):
        piece = piece_of(q, yy)
        beside.append(links.copy(piece, piece, at.sibling()))

    yield from gather_y(at, links, piece_of, ready, also)
    for one in beside:
        one.wait_recv()
    yield


def run(*streams):
    streams = list(streams)
    while streams:
        for stream in list(streams):
            if next(stream, "end") == "end":
                streams.remove(stream)


def first_kernel(
    tokens, w_query, w_key, w_value, w_out, cotangent, gathered, weights, d_att,
    part, half_buf, side_buf, sums, peer_buf, send, recv,
):
    at = Place()
    links = Links(send, recv)
    pack_into(gathered, (at.x, at.z), tokens[...])
    mine = (at.zh, at.y, at.c)
    for i, w in enumerate((w_query, w_key, w_value)):
        weights[mine + (slice(None), slice(i * LOCAL, (i + 1) * LOCAL))] = w[...]
    weights[mine + (slice(None), slice(3 * LOCAL, WCOLS))] = jnp.zeros((WROWS, WCOLS - 3 * LOCAL), BF16)
    greet(
        [at.x_side(1), at.x_side(-1)] + [at.z_peer(k) for k in (1, 2, 3)]
        + [at.y_side(1), at.y_side(-1), at.zh_peer(), at.sibling()]
    )
    token_stream = gather_mp(at, links, gathered)
    weight_stream = gather_dp(at, links, weights)
    next(weight_stream)
    next(token_stream)

    @pl.loop(0, 8)
    def _(i):
        columns = pl.ds(pl.multiple_of(i * 384, 384), 384)
        block = jnp.dot(cotangent[...], w_out[:, columns], preferred_element_type=F32).astype(BF16)
        spot = (lax.div(i, 2), lax.rem(i, 2) * 2)
        pack_into(part, spot, block[:, 0:192])
        pack_into(part, (spot[0], spot[1] + 1), block[:, 192:384])

    def finish(total):
        unpack_into(d_att, 0, total.astype(BF16))

    run(token_stream, weight_stream, reduce_mp(at, links, part, half_buf, side_buf, sums, peer_buf, finish))
    links.finish()


def head_norm(projected):
    mean = jnp.mean(projected, axis=-1, keepdims=True)
    centred = projected - mean
    var = jnp.mean(centred * centred, axis=-1, keepdims=True)
    inverse = lax.rsqrt(var + EPS)
    return (centred * inverse, inverse)


def norm_back(grad_hat, hat, inverse):
    first = jnp.mean(grad_hat, axis=-1, keepdims=True)
    second = jnp.mean(grad_hat * hat, axis=-1, keepdims=True)
    return inverse * (grad_hat - first - hat * second)


def dot(a, b, dims):
    return lax.dot_general(a, b, ((dims[:1], dims[1:]), ((), ())), preferred_element_type=F32)


def middle_kernel(gathered, weights, d_att, attended, terms, normed, qkv, d_qkv):
    for j in range(NX * NZ):
        unpack_into(normed, j * LOCAL, gathered[j])

    @pl.loop(0, ROWS // 32)
    def _(i):
        rows = pl.ds(pl.multiple_of(i * 32, 32), 32)
        whole = normed[rows, :].astype(F32)
        mean = jnp.mean(whole, axis=-1, keepdims=True)
        centred = whole - mean
        var = jnp.mean(centred * centred, axis=-1, keepdims=True)
        normed[rows, :] = (centred * lax.rsqrt(var + EPS)).astype(BF16)

    qkv[...] = jnp.dot(normed[...], weights[...], preferred_element_type=F32)
    scale = HEAD_DIM ** (-0.5)
    for i in range(ROWS // TOK):
        rows = slice(i * TOK, (i + 1) * TOK)
        for h in range(LOCAL // HEAD_DIM):
            cols = slice(h * HEAD_DIM, (h + 1) * HEAD_DIM)
            kcols = slice(LOCAL + h * HEAD_DIM, LOCAL + (h + 1) * HEAD_DIM)
            vcols = slice(2 * LOCAL + h * HEAD_DIM, 2 * LOCAL + (h + 1) * HEAD_DIM)
            q_hat, inv_q = head_norm(qkv[rows, cols])
            k_hat, inv_k = head_norm(qkv[rows, kcols])
            v_low = qkv[rows, vcols].astype(BF16)
            q_low, k_low = q_hat.astype(BF16), k_hat.astype(BF16)
            exps = jnp.exp(dot(q_low, k_low, (1, 1)) * scale)
            probs = exps / jnp.sum(exps, axis=-1, keepdims=True)
            probs_low = probs.astype(BF16)
            attended[rows, cols] = dot(probs_low, v_low, (1, 0)).astype(BF16)
            d_out = d_att[rows, cols]
            d_probs = dot(d_out, v_low, (1, 1))
            inner = jnp.sum(probs * d_probs, axis=-1, keepdims=True)
            d_scores = (probs * (d_probs - inner) * scale).astype(BF16)
            d_qhat = dot(d_scores, k_low, (1, 0))
            d_khat = dot(d_scores, q_low, (0, 0))
            d_value = dot(probs_low, d_out, (0, 0))
            d_qkv[rows, cols] = norm_back(d_qhat, q_hat, inv_q).astype(BF16)
            d_qkv[rows, kcols] = norm_back(d_khat, k_hat, inv_k).astype(BF16)
            d_qkv[rows, vcols] = d_value.astype(BF16)
    d_qkv[:, 3 * LOCAL : WCOLS] = jnp.zeros((ROWS, WCOLS - 3 * LOCAL), BF16)

    @pl.loop(0, 12)
    def _(i):
        span = pl.ds(pl.multiple_of(i * 256, 256), 256)
        terms[span, :] = dot(normed[:, span], d_qkv[...], (0, 0)).astype(BF16)


def last_kernel(
    attended, terms, w_out, cotangent, branch, g_query, g_key, g_value, g_out,
    gathered, att_all, sib_buf, out_buf, in_buf, keep, send_buf, peer_buf,
    o_terms, o_sib, o_out, o_in, o_send, o_peer, o_whole, send, recv,
):
    at = Place()
    links = Links(send, recv)
    pack_into(gathered, (at.x, at.z), attended[...])
    greet(
        [at.x_side(1), at.x_side(-1)] + [at.z_peer(k) for k in (1, 2, 3)]
        + [at.y_side(1), at.y_side(-1), at.zh_peer(), at.sibling()]
    )

    def finish(total):
        for i, out in enumerate((g_query, g_key, g_value)):
            out[...] = total[:, i * LOCAL : (i + 1) * LOCAL]

    def output_stream():
        yield from gather_mp(at, links, gathered)
        for j in range(NX * NZ):
            unpack_into(att_all, j * LOCAL, gathered[j // NZ, j % NZ])

        @pl.loop(0, NY)
        def _(i):
            columns = pl.ds(pl.multiple_of(i * GCOLS, GCOLS), GCOLS)
            block = dot(cotangent[...], att_all[:, columns], (0, 0)).astype(BF16)
            o_terms[0, i] = block[0:WROWS]
            o_terms[1, i] = block[WROWS : 2 * WROWS]

        yield from allreduce_dp(at, links, o_terms, o_sib, o_out, o_in, o_send, o_peer, o_whole)

    run(
        output_stream(),
        reduce_dp(at, links, terms, sib_buf, out_buf, in_buf, keep, send_buf, peer_buf, finish),
    )
    branch[...] = dot(att_all[...], w_out[...], (1, 1)).astype(BF16)
    for c in range(NC):
        for y in range(NY):
            g_out[c * WROWS : (c + 1) * WROWS, y * GCOLS : (y + 1) * GCOLS] = o_whole[c, y].astype(F32)
    links.finish()


def in_vmem(count):
    return [pl.BlockSpec(memory_space=pltpu.VMEM)] * count


def call(kernel, operands, outs, scratch, collective_id=None):
    extra = {} if collective_id is None else dict(collective_id=collective_id, has_side_effects=True)
    return pl.pallas_call(
        kernel,
        out_shape=[jax.ShapeDtypeStruct(shape, kind) for shape, kind in outs],
        in_specs=in_vmem(len(operands)),
        out_specs=in_vmem(len(outs)),
        scratch_shapes=scratch,
        compiler_params=pltpu.CompilerParams(vmem_limit_bytes=48 * 1024 * 1024, **extra),
    )(*operands)


def body(tokens, w_query, w_key, w_value, w_out, cotangent):
    gathered, weights, d_att = call(
        first_kernel,
        (tokens, w_query, w_key, w_value, w_out, cotangent),
        [((NX, NZ, PACK, 128), BF16), ((NZH, NY, NC, WROWS, WCOLS), BF16), ((ROWS, LOCAL), BF16)],
        [
            pltpu.VMEM((NX, NZ, PACK, 128), BF16),
            pltpu.VMEM((2, NZ, HALF, 128), BF16),
            pltpu.VMEM((2, NZ, PACK, 128), BF16),
            pltpu.VMEM((3, PACK, 128), BF16),
            pltpu.VMEM((3, PACK, 128), BF16),
            pltpu.SemaphoreType.DMA((64,)),
            pltpu.SemaphoreType.DMA((64,)),
        ],
        0,
    )
    attended, terms = call(
        middle_kernel,
        (gathered.reshape(NX * NZ, PACK, 128), weights.reshape(-1, WCOLS), d_att),
        [((ROWS, LOCAL), BF16), ((NZH * NY * NC * WROWS, WCOLS), BF16)],
        [
            pltpu.VMEM((ROWS, NX * NZ * LOCAL), BF16),
            pltpu.VMEM((ROWS, WCOLS), F32),
            pltpu.VMEM((ROWS, WCOLS), BF16),
        ],
    )
    slots = 14
    branch, g_query, g_key, g_value, g_out = call(
        last_kernel,
        (attended, terms.reshape(NZH, NY, NC, WROWS, WCOLS), w_out, cotangent),
        [((ROWS, LOCAL), BF16)] + [((WROWS, LOCAL), F32)] * 3 + [((2 * WROWS, NY * GCOLS), F32)],
        [
            pltpu.VMEM((NX, NZ, PACK, 128), BF16),
            pltpu.VMEM((ROWS, NX * NZ * LOCAL), BF16),
            pltpu.VMEM((NY, NZH, WROWS, WCOLS), BF16),
            pltpu.VMEM((slots, WROWS, WCOLS), BF16),
            pltpu.VMEM((slots, WROWS, WCOLS), BF16),
            pltpu.VMEM((NZH, WROWS, WCOLS), F32),
            pltpu.VMEM((NZH, WROWS, WCOLS), BF16),
            pltpu.VMEM((WROWS, WCOLS), BF16),
            pltpu.VMEM((NC, NY, WROWS, GCOLS), BF16),
            pltpu.VMEM((NY, WROWS, GCOLS), BF16),
            pltpu.VMEM((slots, WROWS // 2, GCOLS), BF16),
            pltpu.VMEM((slots, WROWS // 2, GCOLS), BF16),
            pltpu.VMEM((2, WROWS // 2, GCOLS), BF16),
            pltpu.VMEM((2, WROWS // 2, GCOLS), BF16),
            pltpu.VMEM((NC, NY, WROWS, GCOLS), BF16),
            pltpu.SemaphoreType.DMA((112,)),
            pltpu.SemaphoreType.DMA((112,)),
        ],
        1,
    )
    return (branch, g_query, g_key, g_value, g_out)


def solution(mesh):
    return jax.shard_map(
        body,
        mesh=mesh,
        in_specs=(
            P("dp", "mp"),
            P("dp", "mp"),
            P("dp", "mp"),
            P("dp", "mp"),
            P("mp", None),
            P("dp", "mp"),
        ),
        out_specs=(P("dp", "mp"), P("dp", "mp"), P("dp", "mp"), P("dp", "mp"), P("mp", None)),
        check_vma=False,
    )
```
